128 devices in a mesh: grp: 8 (over x, y_lo), sub: 16 (over y_hi, z, core).
Axes of the slice: x: 4, y: 4 (y_hi: 2, y_lo: 2; y = y_hi * 2 + y_lo), z: 4, core: 2. Of those that a mesh axis runs over, the one named last changes fastest.
Arguments:
- h1: bfloat16 [1048576, 256], P(('grp', 'sub')), may hold values from -6 to 6
- h2: bfloat16 [262144, 256], P(('grp', 'sub')), may hold values from -6 to 6
- nbr1: int32 [1048576, 8], P(('grp', 'sub')), may hold values from -1024 to 1024, as said below
- mask1: int32 [1048576, 8], P(('grp', 'sub')), may hold values 0 or 1
- owner: int32 [1048576], P(('grp', 'sub')), may hold values from 0 to 262143, as said below
- nbr2: int32 [262144, 8], P(('grp', 'sub')), may hold values from 0 to 262143, as said below
- mask2: int32 [262144, 8], P(('grp', 'sub')), may hold values 0 or 1
- a1: bfloat16 [256, 256], replicated, may hold values from -0.375 to 0.375
- b1: bfloat16 [256, 256], replicated, may hold values from -0.375 to 0.375
- m1: bfloat16 [256, 256], replicated, may hold values from -0.375 to 0.375
- u1: bfloat16 [256, 256], replicated, may hold values from -0.125 to 0.125
- a_up: bfloat16 [256, 256], replicated, may hold values from -0.375 to 0.375
- m_up: bfloat16 [256, 256], replicated, may hold values from -0.375 to 0.375
- u2: bfloat16 [256, 256], replicated, may hold values from -0.1875 to 0.1875
- a2: bfloat16 [256, 256], replicated, may hold values from -0.375 to 0.375
- b2: bfloat16 [256, 256], replicated, may hold values from -0.375 to 0.375
- m2: bfloat16 [256, 256], replicated, may hold values from -0.375 to 0.375
- v2: bfloat16 [256, 256], replicated, may hold values from -0.125 to 0.125
- a_down: bfloat16 [256, 256], replicated, may hold values from -0.375 to 0.375
- b_down: bfloat16 [256, 256], replicated, may hold values from -0.375 to 0.375
- m_down: bfloat16 [256, 256], replicated, may hold values from -0.375 to 0.375
Outputs:
- h1_out: bfloat16 [1048576, 256], P(('grp', 'sub'))
- h2_out: bfloat16 [262144, 256], P(('grp', 'sub'))
The draws below stay inside these ranges and needn't reach their ends.
Inputs may be any that keep to these rules, and one draw needn't show every extreme that they name: i + nbr1[i, k] lies in 0 to 1048575; column 0 is max(-1024, -i) and column 7 is min(1024, 1048575 - i). owner[r] lies within 256 of r // 4 and in the same aligned block of 32768 rows as r // 4; the first of each device's 8192 rows points 256 below r // 4 and the last 256 above, where that block allows. nbr2[n, k] lies within 256 of n and in the same aligned block of 32768 rows as n; column 0 and column 7 reach 256 below and above where that block allows.
All inputs are finite; a program needn't handle non-finite values. No bound on the sum of `mask1` or of `mask2` on one device may be relied on, other than what follows from the above.
Results may differ from the reference program's by a relative error of at most 0.015.
Values may be sent and summed in bfloat16 or wider, within the bound.
No kernel may reach another device: no remote copies, remote signals or barrier semaphores. Data moves between devices by JAX's collectives and lax.ppermute only.
A program may use at most 128 MiB of HBM per device.

```python
import jax
import jax.numpy as jnp
from jax import lax

H = 256
K = 8
K2 = 8
N1_DEV = 8192
R1 = 1024
R2 = 256
N1 = 1048576
N2 = 262144
N2G = 32768


def draw_nbr1(key, part):
    key = jax.random.fold_in(key, 11)
    rows = jnp.arange(N1, dtype=jnp.int32)[:, None]
    offsets = jax.random.randint(key, (N1, K), -R1, R1 + 1, dtype=jnp.int32)
    offsets = offsets.at[:, 0].set(-R1).at[:, K - 1].set(R1)
    target = jnp.clip(rows + offsets, 0, N1 - 1)
    return (target - rows).astype(jnp.int32)


def draw_owner(key, part):
    key = jax.random.fold_in(key, 23)
    rows = jnp.arange(N1, dtype=jnp.int32)
    local = rows % N1_DEV
    center = rows // 4
    lowest = center // N2G * N2G
    offsets = jax.random.randint(key, (N1,), -R2, R2 + 1, dtype=jnp.int32)
    offsets = jnp.where(local == 0, -R2, jnp.where(local == N1_DEV - 1, R2, offsets))
    return jnp.clip(center + offsets, lowest, lowest + N2G - 1).astype(jnp.int32)


def draw_nbr2(key, part):
    key = jax.random.fold_in(key, 37)
    rows = jnp.arange(N2, dtype=jnp.int32)[:, None]
    offsets = jax.random.randint(key, (N2, K2), -R2, R2 + 1, dtype=jnp.int32)
    offsets = offsets.at[:, 0].set(-R2).at[:, K2 - 1].set(R2)
    lowest = rows // N2G * N2G
    return jnp.clip(rows + offsets, lowest, lowest + N2G - 1).astype(jnp.int32)


def plant(drawn, rng, low, high):
    spot = [jax.random.randint(jax.random.fold_in(rng, axis), (), 0, length) for axis, length in enumerate(drawn.shape)]
    main_axis = drawn.shape.index(max(drawn.shape))
    beside = spot[:main_axis] + [(spot[main_axis] + 1) % drawn.shape[main_axis]] + spot[main_axis + 1:]
    return drawn.at[tuple(spot)].set(low).at[tuple(beside)].set(high)


def levels(own_key, shape, split, least, high):
    def one(axis_at, shards_of):
        draws = jax.random.uniform(jax.random.fold_in(jax.random.fold_in(own_key, 6), axis_at), (shards_of,), jnp.float32, least / len(split), high / len(split))
        return jnp.repeat(jnp.exp(draws), shape[axis_at] // shards_of).reshape((-1,) + (1,) * (len(shape) - axis_at - 1))

    level = one(*split[0])
    for cut in split[1:]:
        level = level * one(*cut)
    return level


def noise(rng, extent, deviation, most, shards=(), held_as=jnp.bfloat16):
    gain = levels(rng, extent, shards, -0.22, 0.18) if shards else 1.0
    drawn = jax.random.normal(rng, extent, jnp.float32) * deviation * gain
    return jnp.minimum(jnp.maximum(drawn, -most), most).astype(held_as)


def setup_inputs(seed: int = 0) -> dict:
    splits = jax.random.split(jax.random.key(seed), 22)
    h1 = noise(splits[0], (N1, H), 1.0, 6.0, ((0, 128),))
    h2 = noise(splits[1], (N2, H), 1.0, 6.0, ((0, 128),))
    nbr1 = draw_nbr1(jax.random.fold_in(splits[21], 71), 0)
    mask1 = plant((jax.random.randint(splits[3], (N1, K), 0, 4) < 3).astype(jnp.int32), jax.random.fold_in(splits[3], 1), 0, 1)
    owner = draw_owner(jax.random.fold_in(splits[21], 71), 0)
    nbr2 = draw_nbr2(jax.random.fold_in(splits[21], 71), 0)
    mask2 = plant((jax.random.randint(splits[6], (N2, K2), 0, 4) < 3).astype(jnp.int32), jax.random.fold_in(splits[6], 1), 0, 1)
    a1 = noise(splits[7], (H, H), H ** -0.5, 0.375)
    b1 = noise(splits[8], (H, H), H ** -0.5, 0.375)
    m1 = noise(splits[9], (H, H), H ** -0.5, 0.375)
    u1 = noise(splits[10], (H, H), (K * H) ** -0.5, 0.125)
    a_up = noise(splits[11], (H, H), H ** -0.5, 0.375)
    m_up = noise(splits[12], (H, H), H ** -0.5, 0.375)
    u2 = noise(splits[13], (H, H), (4 * H) ** -0.5, 0.1875)
    a2 = noise(splits[14], (H, H), H ** -0.5, 0.375)
    b2 = noise(splits[15], (H, H), H ** -0.5, 0.375)
    m2 = noise(splits[16], (H, H), H ** -0.5, 0.375)
    v2 = noise(splits[17], (H, H), (K2 * H) ** -0.5, 0.125)
    a_down = noise(splits[18], (H, H), H ** -0.5, 0.375)
    b_down = noise(splits[19], (H, H), H ** -0.5, 0.375)
    m_down = noise(splits[20], (H, H), H ** -0.5, 0.375)
    return {"h1": h1, "h2": h2, "nbr1": nbr1, "mask1": mask1, "owner": owner, "nbr2": nbr2, "mask2": mask2, "a1": a1, "b1": b1, "m1": m1, "u1": u1, "a_up": a_up, "m_up": m_up, "u2": u2, "a2": a2, "b2": b2, "m2": m2, "v2": v2, "a_down": a_down, "b_down": b_down, "m_down": m_down}


def normalize(x):
    center = x - lax.optimization_barrier(jnp.mean(x, axis=-1, keepdims=True))
    spread = lax.optimization_barrier(jnp.mean(center * center, axis=-1, keepdims=True))
    return center * lax.rsqrt(spread + 1e-05)

def edge_sum(proj_src, proj_dst, index, mask, w_msg):
    nodes, width = proj_dst.shape
    degree = index.shape[1]
    block = min(512, nodes)
    count = nodes // block

    def one(step):
        start = step * block
        idx = lax.dynamic_slice_in_dim(index, start, block, 0)
        live = lax.dynamic_slice_in_dim(mask, start, block, 0).astype(jnp.float32)
        dst = lax.dynamic_slice_in_dim(proj_dst, start, block, 0)
        pre = jnp.take(proj_src, idx.reshape(-1), axis=0).reshape(block, degree, width) + dst[:, None, :]
        act = jax.nn.silu(pre).astype(jnp.bfloat16).reshape(block * degree, width)
        out = normalize(jnp.dot(act, w_msg, preferred_element_type=jnp.float32)).reshape(block, degree, width)
        return lax.optimization_barrier(jnp.sum(out * live[:, :, None], axis=1))
    steps = jnp.arange(count, dtype=jnp.int32)
    return lax.map(one, steps).reshape(nodes, width)

def reference(h1, h2, nbr1, mask1, owner, nbr2, mask2, a1, b1, m1, u1, a_up, m_up, u2, a2, b2, m2, v2, a_down, b_down, m_down):
    src1 = jnp.dot(h1, a1, preferred_element_type=jnp.float32)
    dst1 = jnp.dot(h1, b1, preferred_element_type=jnp.float32)
    rows = jnp.arange(N1, dtype=jnp.int32)[:, None]
    index1 = (rows + nbr1).astype(jnp.int32)
    agg1 = edge_sum(src1, dst1, index1, mask1, m1).astype(jnp.bfloat16)
    h1a = (h1.astype(jnp.float32) + jnp.dot(agg1, u1, preferred_element_type=jnp.float32)).astype(jnp.bfloat16)
    up_act = jax.nn.silu(jnp.dot(h1a, a_up, preferred_element_type=jnp.float32)).astype(jnp.bfloat16)
    up_msg = normalize(jnp.dot(up_act, m_up, preferred_element_type=jnp.float32)).astype(jnp.bfloat16)
    up_agg = jax.ops.segment_sum(up_msg.astype(jnp.float32), owner, num_segments=N2).astype(jnp.bfloat16)
    h2a = (h2.astype(jnp.float32) + jnp.dot(up_agg, u2, preferred_element_type=jnp.float32)).astype(jnp.bfloat16)
    src2 = jnp.dot(h2a, a2, preferred_element_type=jnp.float32)
    dst2 = jnp.dot(h2a, b2, preferred_element_type=jnp.float32)
    agg2 = edge_sum(src2, dst2, nbr2, mask2, m2).astype(jnp.bfloat16)
    h2_out = (h2a.astype(jnp.float32) + jnp.dot(agg2, v2, preferred_element_type=jnp.float32)).astype(jnp.bfloat16)
    parent = jnp.take(h2_out, owner, axis=0)
    pre = jnp.dot(parent, a_down, preferred_element_type=jnp.float32) + jnp.dot(h1a, b_down, preferred_element_type=jnp.float32)
    down_act = jax.nn.silu(pre).astype(jnp.bfloat16)
    down = normalize(jnp.dot(down_act, m_down, preferred_element_type=jnp.float32))
    h1_out = (h1a.astype(jnp.float32) + down).astype(jnp.bfloat16)
    return (h1_out, h2_out)
```

```python
import functools

import jax
import jax.numpy as jnp
from jax import lax
from jax.experimental import pallas as pl
from jax.experimental.pallas import tpu as pltpu
from jax.sharding import PartitionSpec as P

F32 = jnp.float32
BF16 = jnp.bfloat16
W = 256
L = 128
K = 8
C = 128
UNROLL = 4
PIECE = 16
DEAD = -10000.0
EPS = 1e-05
VMEM_BYTES = 56 * 2**20
REACH1 = 1024
REACH2 = 256


def mm(x, y):
    return jnp.dot(x, y, preferred_element_type=F32)


def half(ref):
    return (ref[...].astype(F32) * 0.5).astype(BF16)


def centered(ref):
    w = ref[...].astype(F32)
    return (w - jnp.mean(w, axis=1, keepdims=True)).astype(BF16)


def act_of(y):
    return y + y * jnp.tanh(y)


def ones_block():
    return jnp.full((L, L), 1.0 / W, BF16)


def scale_of(y):
    lo = y[:, :L]
    hi = y[:, L:]
    s = (lo * lo + hi * hi).astype(BF16)
    return lax.rsqrt(mm(s, ones_block()) + EPS)


def store_table(tab, row0, p):
    n = p.shape[0]
    tab[pl.ds(2 * row0, n, stride=2), :] = p[:, :L]
    tab[pl.ds(2 * row0 + 1, n, stride=2), :] = p[:, L:]


def build_table(tab, ext, a, rows):
    step = 256

    def one(b, carry):
        r = pl.multiple_of(b * step, step)
        store_table(tab, r, mm(ext[pl.ds(r, step), :], a))
        return carry

    lax.fori_loop(0, rows // step, one, 0)
    tab[pl.ds(2 * rows, 8), :] = jnp.full((8, L), DEAD, F32)


def edge_loop(nc, idx_vm, slots, sems, bufs, tab, dst, mc, z, post, finish):
    def fetch(c, s):
        return pltpu.make_async_copy(idx_vm.at[jnp.minimum(c, nc - 1)], slots[s], sems.at[s])

    def gather(slot, buf, k):
        for i in range(C):
            j = slot[k, i]
            buf[pl.ds(2 * (k * C + i), 2), :] = tab[pl.ds(j, 2), :]

    def piece(buf, node, i0, zrow):
        d = dst[pl.ds(node + i0, PIECE), :]
        d0 = d[:, :L]
        d1 = d[:, L:]
        acts = []
        for k in range(K):
            base = 2 * (k * C + i0)
            y0 = buf[pl.ds(base, PIECE, stride=2), :] + d0
            y1 = buf[pl.ds(base + 1, PIECE, stride=2), :] + d1
            acts.append(jnp.concatenate([act_of(y0), act_of(y1)], axis=1).astype(BF16))
        w = scale_of(mm(jnp.concatenate(acts, axis=0), mc[...]))
        acc0 = acc1 = None
        for k in range(K):
            wk = w[k * PIECE : (k + 1) * PIECE]
            a = acts[k].astype(F32)
            t0 = a[:, :L] * wk
            t1 = a[:, L:] * wk
            acc0 = t0 if k == 0 else acc0 + t0
            acc1 = t1 if k == 0 else acc1 + t1
        z[pl.ds(zrow + i0, PIECE), :] = jnp.concatenate([acc0, acc1], axis=1).astype(BF16)

    for s in range(UNROLL):
        fetch(s, s).start()
    fetch(0, 0).wait()
    for k in range(K):
        gather(slots[0], bufs[0], k)
    fetch(UNROLL, 0).start()

    def body(t, carry):
        for g in range(UNROLL):
            c = t * UNROLL + g
            nxt = (g + 1) % UNROLL
            node = pl.multiple_of(c * C, C)
            fetch(c + 1, nxt).wait()
            for p in range(C // PIECE):
                gather(slots[nxt], bufs[(g + 1) % 2], p)
                piece(bufs[g % 2], node, p * PIECE, g * C)
            fetch(c + 1 + UNROLL, nxt).start()
            post(node, g)
        finish(t)
        return carry

    lax.fori_loop(0, nc // UNROLL, body, 0)
    for s in range(UNROLL):
        fetch(0, s).wait()


def level1_kernel(
    segs, widths, prev_rows, next_rows, first, base_ref, *refs
):
    ns = len(segs)
    refs = list(refs)
    nbr = [refs.pop(0) for _ in range(ns)]
    mask = [refs.pop(0) for _ in range(ns)]
    owner = refs.pop(0)
    h1 = refs.pop(0)
    prev = refs.pop(0) if prev_rows else None
    nxt = refs.pop(0) if next_rows else None
    a1, b1, m1, u1, a_up, m_up = [refs.pop(0) for _ in range(6)]
    if not first:
        refs.pop(0)
    h1a = refs.pop(0)
    part = refs.pop(0)
    if prev_rows:
        send_lo = refs.pop(0)
        send_hi = refs.pop(0)
    (ext, tab, dst, idx_vm, s0, s1, s2, s3, r0, r1, z, msg, out, mc, mu, ma, mupc, fsem, csem) = refs

    seg_nodes = widths
    nodes = ns * seg_nodes
    rows = ext.shape[0]
    seg_rows = rows // ns
    loads = []
    for q, start in enumerate(segs):
        lo = start - REACH1
        hi = start + seg_nodes + REACH1
        at = q * seg_rows
        if lo < 0:
            loads.append((prev, 0, at, REACH1))
            at += REACH1
            lo = 0
        end = min(hi, h1.shape[0])
        loads.append((h1, lo, at, end - lo))
        at += end - lo
        if hi > end:
            loads.append((nxt, 0, at, REACH1))
    copies = [
        pltpu.make_async_copy(src.at[pl.ds(off, n), :], ext.at[pl.ds(at, n), :], csem.at[i])
        for i, (src, off, at, n) in enumerate(loads)
    ]
    for cp in copies:
        cp.start()

    lane = lax.broadcasted_iota(jnp.int32, (K, L), 1)
    for q in range(ns):
        for c in range(seg_nodes // C):
            cols = slice(c * C, (c + 1) * C)
            row = nbr[q][:, cols] + (lane + (q * seg_rows + REACH1 + c * C))
            idx_vm[q * (seg_nodes // C) + c] = 2 * jnp.where(mask[q][:, cols] > 0, row, rows)
    mcv = centered(m1)
    mc[...] = mcv
    mu[...] = mm(mcv, u1[...]).astype(BF16)
    ma[...] = half(a_up)
    mupc[...] = centered(m_up)
    part[...] = jnp.zeros(part.shape, F32)
    for cp in copies:
        cp.wait()
    build_table(tab, ext, half(a1), rows)
    bh = half(b1)
    for q in range(ns):
        for b in range(seg_nodes // 256):
            src = q * seg_rows + REACH1 + b * 256
            dst[pl.ds(q * seg_nodes + b * 256, 256), :] = mm(ext[pl.ds(src, 256), :], bh)

    def own(node):
        return node if ns == 1 else node + (node // seg_nodes) * (seg_rows - seg_nodes)

    def post(node, g):
        src = pl.multiple_of(own(node) + REACH1, C)
        h = ext[pl.ds(src, C), :].astype(F32) + mm(z[pl.ds(g * C, C), :], mu[...])
        hb = h.astype(BF16)
        out[pl.ds(node, C), :] = hb
        y = mm(act_of(mm(hb, ma[...])).astype(BF16), mupc[...])
        w = scale_of(y)
        msg[pl.ds(g * C, C), :] = jnp.concatenate([y[:, :L] * w, y[:, L:] * w], axis=1).astype(BF16)

    span = UNROLL * C
    win = span // 4 + 2 * REACH2
    part_rows = seg_nodes // 4 + 2 * REACH2

    def finish(t):
        per = seg_nodes // span
        q = t // per
        inner = t - q * per
        seg_start = segs[0] if ns == 1 else segs[0] + q * (segs[1] - segs[0])
        lowest = base_ref[0] + (seg_start + inner * span) // 4 - REACH2
        ids = lax.broadcasted_iota(jnp.int32, (win, L), 0) + lowest
        orow = (seg_start + inner * span) // L
        hot = []
        for j in range(UNROLL):
            ow = owner[pl.ds(orow + j, 1), :]
            hot.append(jnp.where(ids == ow, 1.0, 0.0).astype(BF16))
        at = pl.multiple_of(q * part_rows + inner * (span // 4), C)
        part[pl.ds(at, win), :] += mm(jnp.concatenate(hot, axis=1), msg[...])

    edge_loop(
        nodes // C, idx_vm, (s0, s1, s2, s3), fsem, (r0, r1), tab, dst, mc, z, post, finish
    )
    stores = [
        pltpu.make_async_copy(
            out.at[pl.ds(q * seg_nodes, seg_nodes), :], h1a.at[pl.ds(start, seg_nodes), :], csem.at[q]
        )
        for q, start in enumerate(segs)
    ]
    for cp in stores:
        cp.start()
    if prev_rows:
        n = 2 * REACH2
        send_lo[...] = part[pl.ds(0, n), :].astype(BF16)
        send_hi[...] = part[pl.ds(part.shape[0] - n, n), :].astype(BF16)
    for cp in stores:
        cp.wait()


def vmem():
    return pl.BlockSpec(memory_space=pltpu.VMEM)


def anyspace():
    return pl.BlockSpec(memory_space=pl.ANY)


def gather_scratch(rows, nodes):
    return [
        pltpu.VMEM((2 * rows + 8, L), F32),
        pltpu.VMEM((nodes, W), F32),
        pltpu.VMEM((nodes // C, K, L), jnp.int32),
        *[pltpu.SMEM((K, L), jnp.int32) for _ in range(UNROLL)],
        *[pltpu.VMEM((2 * K * C, L), F32) for _ in range(2)],
        pltpu.VMEM((UNROLL * C, W), BF16),
    ]


def level1(segs, base, nbr_t, mask_t, owner2, h1, halo, weights, carry, nodes1):
    ns = len(segs)
    width = 2048
    nodes = ns * width
    rows = nodes + ns * 2 * REACH1
    part_rows = ns * (width // 4 + 2 * REACH2)
    first = carry is None
    ends = halo is not None
    cut = [pl.BlockSpec((K, width), functools.partial(lambda b, t: (0, b), s // width)) for s in segs]
    args = [base] + [nbr_t] * ns + [mask_t] * ns + [owner2, h1]
    specs = [pl.BlockSpec(memory_space=pltpu.SMEM)] + cut + cut + [vmem(), anyspace()]
    if ends:
        args += list(halo)
        specs += [anyspace()] * 2
    args += list(weights)
    specs += [vmem()] * len(weights)
    aliases = {}
    if not first:
        aliases = {len(args): 0}
        args.append(carry)
        specs.append(anyspace())
    shapes = [jax.ShapeDtypeStruct((nodes1, W), BF16), jax.ShapeDtypeStruct((part_rows, W), F32)]
    out_specs = [anyspace(), vmem()]
    if ends:
        shapes += [jax.ShapeDtypeStruct((2 * REACH2, W), BF16)] * 2
        out_specs += [vmem()] * 2
    edges = nodes * K
    return pl.pallas_call(
        functools.partial(level1_kernel, segs, width, ends, ends, first),
        grid=(1,),
        out_shape=shapes,
        in_specs=specs,
        out_specs=out_specs,
        input_output_aliases=aliases,
        scratch_shapes=[
            pltpu.VMEM((rows, W), BF16),
            *gather_scratch(rows, nodes),
            pltpu.VMEM((UNROLL * C, W), BF16),
            pltpu.VMEM((nodes, W), BF16),
            *[pltpu.VMEM((W, W), BF16) for _ in range(4)],
            pltpu.SemaphoreType.DMA((UNROLL,)),
            pltpu.SemaphoreType.DMA((4,)),
        ],
        compiler_params=pltpu.CompilerParams(vmem_limit_bytes=VMEM_BYTES),
        cost_estimate=pl.CostEstimate(
            flops=4 * edges * W * W, bytes_accessed=rows * W * 4, transcendentals=edges * W
        ),
        name="level1_ends" if ends else "level1_middle",
    )(*args)


def level2_kernel(chunks, first, base_ref, nbr, mask, *refs):
    refs = list(refs)
    if first:
        pe, p1, p2, from_lo, from_hi, h2, lo2, hi2, u2 = [refs.pop(0) for _ in range(9)]
    else:
        h2x_in = refs.pop(0)
    a2, b2, m2, v2 = [refs.pop(0) for _ in range(4)]
    if not first:
        refs.pop(0)
    h2o = refs.pop(0)
    if first:
        h2x, edge_lo, edge_hi = [refs.pop(0) for _ in range(3)]
    (tab, dst, idx_vm, s0, s1, s2, s3, r0, r1, z, out, mc, mv, fsem, csem) = refs
    n2 = h2o.shape[0]
    rows = n2 + 2 * REACH2
    S = 2 * REACH2
    if first:
        u = u2[...]
        pieces = [
            pe[pl.ds(0, S), :] + from_lo[...].astype(F32),
            pe[pl.ds(S, S), :] + p1[pl.ds(0, S), :],
            p1[pl.ds(S, S), :] + p2[pl.ds(0, S), :],
            p2[pl.ds(S, S), :] + pe[pl.ds(2 * S, S), :],
            pe[pl.ds(3 * S, S), :] + from_hi[...].astype(F32),
        ]
        for q, piece in enumerate(pieces):
            d = mm(piece.astype(BF16), u)
            for hf in range(2):
                at = q * S + hf * REACH2
                if at == 0:
                    src = lo2[...]
                elif at == rows - REACH2:
                    src = hi2[...]
                else:
                    src = h2[pl.ds(at - REACH2, REACH2), :]
                dd = d[hf * REACH2 : (hf + 1) * REACH2]
                h2x[pl.ds(at, REACH2), :] = (src.astype(F32) + dd).astype(BF16)
    else:
        h2x = h2x_in
    lane = lax.broadcasted_iota(jnp.int32, (K, L), 1)
    base = base_ref[0]
    for n, c in enumerate(chunks):
        cols = slice(c * C, (c + 1) * C)
        row = nbr[:, cols] - (base - REACH2)
        idx_vm[n] = 2 * jnp.where(mask[:, cols] > 0, row, rows)
    mcv = centered(m2)
    mc[...] = mcv
    mv[...] = mm(mcv, v2[...]).astype(BF16)
    build_table(tab, h2x, half(a2), rows)
    bh = half(b2)
    for n, c in enumerate(chunks):
        dst[pl.ds(n * C, C), :] = mm(h2x[pl.ds(REACH2 + c * C, C), :], bh)

    gap = chunks[0]
    jump = [n for n, c in enumerate(chunks) if c != gap + n]

    def own(node):
        if jump:
            return node + jnp.where(node >= jump[0] * C, (chunks[jump[0]] - jump[0]) * C, 0)
        return node + gap * C

    def post(node, g):
        src = pl.multiple_of(own(node) + REACH2, C)
        h = h2x[pl.ds(src, C), :].astype(F32) + mm(z[pl.ds(g * C, C), :], mv[...])
        out[pl.ds(node, C), :] = h.astype(BF16)

    edge_loop(
        len(chunks), idx_vm, (s0, s1, s2, s3), fsem, (r0, r1), tab, dst, mc, z, post, lambda t: None
    )
    if first:
        edge_lo[...] = out[pl.ds(0, REACH2), :]
        edge_hi[...] = out[pl.ds(REACH2, REACH2), :]
        spans = [(0, 0, REACH2), (REACH2, n2 - REACH2, REACH2)]
    else:
        spans = [(0, gap * C, len(chunks) * C)]
    stores = [
        pltpu.make_async_copy(out.at[pl.ds(s, n), :], h2o.at[pl.ds(d, n), :], csem.at[i])
        for i, (s, d, n) in enumerate(spans)
    ]
    for cp in stores:
        cp.start()
    for cp in stores:
        cp.wait()


def level2(chunks, base, nbr_t, mask_t, head, weights, carry, nodes2):
    first = carry is None
    args = [base, nbr_t, mask_t, *head, *weights]
    specs = [pl.BlockSpec(memory_space=pltpu.SMEM)] + [vmem()] * (len(args) - 1)
    aliases = {}
    if not first:
        aliases = {len(args): 0}
        args.append(carry)
        specs.append(anyspace())
    rows = nodes2 + 2 * REACH2
    shapes = [jax.ShapeDtypeStruct((nodes2, W), BF16)]
    out_specs = [anyspace()]
    if first:
        shapes += [
            jax.ShapeDtypeStruct((rows, W), BF16),
            jax.ShapeDtypeStruct((REACH2, W), BF16),
            jax.ShapeDtypeStruct((REACH2, W), BF16),
        ]
        out_specs += [vmem()] * 3
    nodes = len(chunks) * C
    return pl.pallas_call(
        functools.partial(level2_kernel, chunks, first),
        out_shape=shapes,
        in_specs=specs,
        out_specs=out_specs,
        input_output_aliases=aliases,
        scratch_shapes=[
            *gather_scratch(rows, nodes),
            pltpu.VMEM((nodes, W), BF16),
            pltpu.VMEM((W, W), BF16),
            pltpu.VMEM((W, W), BF16),
            pltpu.SemaphoreType.DMA((UNROLL,)),
            pltpu.SemaphoreType.DMA((2,)),
        ],
        compiler_params=pltpu.CompilerParams(vmem_limit_bytes=VMEM_BYTES),
        cost_estimate=pl.CostEstimate(
            flops=4 * nodes * K * W * W, bytes_accessed=rows * W * 4, transcendentals=nodes * K * W
        ),
        name="level2_ends" if first else "level2_middle",
    )(*args)


DOWN = 512


def down_kernel(base_ref, owner, h1a, h2o, lo, hi, a_down, b_down, m_down, o_ref, pd, bd, mdc):
    t = pl.program_id(0)
    n2 = h2o.shape[0]

    @pl.when(t == 0)
    def _():
        a = half(a_down)
        pd[pl.ds(0, REACH2), :] = mm(lo[...], a).astype(BF16)
        for b in range(n2 // 256):
            pd[pl.ds(REACH2 + b * 256, 256), :] = mm(h2o[pl.ds(b * 256, 256), :], a).astype(BF16)
        pd[pl.ds(REACH2 + n2, REACH2), :] = mm(hi[...], a).astype(BF16)
        bd[...] = half(b_down)
        mdc[...] = centered(m_down)

    win = DOWN // 4 + 2 * REACH2
    start = t * (DOWN // 4)
    lowest = base_ref[0] + start - REACH2
    lane = lax.broadcasted_iota(jnp.int32, (L, L), 1)
    table = pd[pl.ds(pl.multiple_of(start, L), win), :]
    for j in range(DOWN // L):
        ow = owner[pl.ds(t * (DOWN // L) + j, 1), :] - lowest
        col = jnp.transpose(jnp.broadcast_to(ow.astype(F32), (L, L))).astype(jnp.int32)
        hot = jnp.concatenate(
            [jnp.where(col == lane + q * L, 1.0, 0.0).astype(BF16) for q in range(win // L)], axis=1
        )
        hb = h1a[pl.ds(j * L, L), :]
        y = mm(hot, table) + mm(hb, bd[...])
        d = mm(act_of(y).astype(BF16), mdc[...])
        w = scale_of(d)
        ln = jnp.concatenate([d[:, :L] * w, d[:, L:] * w], axis=1)
        o_ref[pl.ds(j * L, L), :] = (hb.astype(F32) + ln).astype(BF16)


def down(base, owner2, h1a, h2o, lo, hi, a_down, b_down, m_down):
    nodes1 = h1a.shape[0]
    n2 = h2o.shape[0]

    def whole(shape):
        return pl.BlockSpec(shape, lambda t: (0, 0))

    block = pl.BlockSpec((DOWN, W), lambda t: (t, 0))
    return pl.pallas_call(
        down_kernel,
        grid=(nodes1 // DOWN,),
        out_shape=jax.ShapeDtypeStruct((nodes1, W), BF16),
        in_specs=[
            pl.BlockSpec(memory_space=pltpu.SMEM),
            whole(owner2.shape),
            block,
            whole((n2, W)),
            whole((REACH2, W)),
            whole((REACH2, W)),
            whole((W, W)),
            whole((W, W)),
            whole((W, W)),
        ],
        out_specs=block,
        scratch_shapes=[
            pltpu.VMEM((n2 + 2 * REACH2, W), BF16),
            pltpu.VMEM((W, W), BF16),
            pltpu.VMEM((W, W), BF16),
        ],
        compiler_params=pltpu.CompilerParams(vmem_limit_bytes=VMEM_BYTES),
        cost_estimate=pl.CostEstimate(
            flops=10 * nodes1 * W * W, bytes_accessed=nodes1 * W * 4, transcendentals=nodes1 * W
        ),
        name="down",
    )(base, owner2, h1a, h2o, lo, hi, a_down, b_down, m_down)


def swap(to_next, to_prev, axis):
    count = lax.axis_size(axis)
    ends = count - 1
    from_prev = lax.ppermute(to_next, axis, [(i, (i + 1) % count) for i in range(ends)])
    from_next = lax.ppermute(to_prev, axis, [((i + 1) % count, i) for i in range(ends)])
    return from_prev, from_next


def shards(
    h1,
    h2,
    nbr1,
    mask1,
    owner,
    nbr2,
    mask2,
    a1,
    b1,
    m1,
    u1,
    a_up,
    m_up,
    u2,
    a2,
    b2,
    m2,
    v2,
    a_down,
    b_down,
    m_down,
):
    nodes1 = h1.shape[0]
    nodes2 = h2.shape[0]
    device = lax.axis_index("grp") * lax.axis_size("sub") + lax.axis_index("sub")
    base = jnp.reshape(device * nodes2, (1,)).astype(jnp.int32)
    nbr1_t, mask1_t, nbr2_t, mask2_t = nbr1.T, mask1.T, nbr2.T, mask2.T
    owner2 = owner.reshape(nodes1 // L, L)
    halo1 = swap(h1[nodes1 - REACH1 :], h1[:REACH1], ("grp", "sub"))
    halo2 = swap(h2[nodes2 - REACH2 :], h2[:REACH2], "sub")
    w1 = (a1, b1, m1, u1, a_up, m_up)
    q = nodes1 // 4

    def one(segs, halo, carry):
        return level1(segs, base, nbr1_t, mask1_t, owner2, h1, halo, w1, carry, nodes1)

    h1a, part1 = one((q,), None, None)
    h1a, part_e, send_lo, send_hi = one((0, 3 * q), halo1, h1a)
    from_lo, from_hi = swap(send_hi, send_lo, "sub")
    h1a, part2 = one((2 * q,), None, h1a)
    w2 = (a2, b2, m2, v2)
    nc2 = nodes2 // C
    head = (part_e, part1, part2, from_lo, from_hi, h2, *halo2, u2)
    h2o, h2x, edge_lo, edge_hi = level2(
        (0, 1, nc2 - 2, nc2 - 1), base, nbr2_t, mask2_t, head, w2, None, nodes2
    )
    lo, hi = swap(edge_hi, edge_lo, "sub")
    (h2_out,) = level2(tuple(range(2, nc2 - 2)), base, nbr2_t, mask2_t, (h2x,), w2, h2o, nodes2)
    h1_out = down(base, owner2, h1a, h2_out, lo, hi, a_down, b_down, m_down)
    return (h1_out, h2_out)


def solution(mesh):
    split = P(("grp", "sub"), None)
    return jax.shard_map(
        shards,
        mesh=mesh,
        in_specs=(split, split, split, split, P(("grp", "sub")), split, split) + (P(),) * 14,
        out_specs=(split, split),
        check_vma=False,
    )
```

```python
import functools

import jax
import jax.numpy as jnp
from jax import lax
from jax.experimental import pallas as pl
from jax.experimental.pallas import tpu as pltpu
from jax.sharding import PartitionSpec as P

F32 = jnp.float32
BF16 = jnp.bfloat16
W = 256
L = 128
K = 8
C = 128
UNROLL = 4
HALF = 2
PIECE = 32
DEAD = -10000.0
EPS = 1e-05
VMEM_BYTES = 56 * 2**20
REACH1 = 1024
REACH2 = 256


def mm(x, y):
    return jnp.dot(x, y, preferred_element_type=F32)


def half(ref):
    return (ref[...].astype(F32) * 0.5).astype(BF16)


def centered(ref):
    w = ref[...].astype(F32)
    return (w - jnp.mean(w, axis=1, keepdims=True)).astype(BF16)


def act_of(y):
    return y + y * jnp.tanh(y)


def ones_block():
    return jnp.full((L, L), 1.0 / W, BF16)


def scale_of(y):
    lo = y[:, :L]
    hi = y[:, L:]
    s = jnp.sum(lo * lo + hi * hi, axis=1, keepdims=True)
    return lax.rsqrt(s * (1.0 / W) + EPS)


def store_table(tab, row0, p):
    n = p.shape[0]
    tab[pl.ds(2 * row0, n, stride=2), :] = p[:, :L]
    tab[pl.ds(2 * row0 + 1, n, stride=2), :] = p[:, L:]


def build_table(tab, ext, a, rows):
    step = 1024 if rows % 1024 == 0 else 512

    def one(b, carry):
        r = pl.multiple_of(b * step, step)
        store_table(tab, r, mm(ext[pl.ds(r, step), :], a))
        return carry

    lax.fori_loop(0, rows // step, one, 0)
    tab[pl.ds(2 * rows, 8), :] = jnp.full((8, L), DEAD, F32)


def build_dst(dst, ext, at, b, rows):
    step = 1024

    def one(i, carry):
        r = pl.multiple_of(i * step, step)
        dst[pl.ds(r, step), :] = mm(ext[pl.ds(at + r, step), :], b)
        return carry

    lax.fori_loop(0, rows // step, one, 0)


def edge_loop(nc, idx_vm, slots, sems, bufs, tab, dst, mc, z, post, finish):
    def fetch(c, s):
        return pltpu.make_async_copy(idx_vm.at[jnp.minimum(c, nc - 1)], slots[s], sems.at[s])

    def gather(slot, buf, k):
        for i in range(C):
            j = slot[k, i]
            buf[pl.ds(2 * (k * C + i), 2), :] = tab[pl.ds(j, 2), :]

    def piece(buf, node, i0, zrow):
        d = dst[pl.ds(node + i0, PIECE), :]
        d0 = d[:, :L]
        d1 = d[:, L:]
        acts = []
        for k in range(K):
            base = 2 * (k * C + i0)
            y0 = buf[pl.ds(base, PIECE, stride=2), :] + d0
            y1 = buf[pl.ds(base + 1, PIECE, stride=2), :] + d1
            acts.append(jnp.concatenate([act_of(y0), act_of(y1)], axis=1).astype(BF16))
        w = scale_of(mm(jnp.concatenate(acts, axis=0), mc[...]))
        acc0 = acc1 = None
        for k in range(K):
            wk = w[k * PIECE : (k + 1) * PIECE]
            a = acts[k].astype(F32)
            t0 = a[:, :L] * wk
            t1 = a[:, L:] * wk
            acc0 = t0 if k == 0 else acc0 + t0
            acc1 = t1 if k == 0 else acc1 + t1
        z[pl.ds(zrow + i0, PIECE), :] = jnp.concatenate([acc0, acc1], axis=1).astype(BF16)

    z[...] = jnp.zeros(z.shape, BF16)
    for s in range(UNROLL):
        fetch(s, s).start()
    fetch(0, 0).wait()
    for k in range(K):
        gather(slots[0], bufs[0], k)
    fetch(UNROLL, 0).start()

    def body(t, carry):
        for g in range(UNROLL):
            c = t * UNROLL + g
            nxt = (g + 1) % UNROLL
            node = pl.multiple_of(c * C, C)
            if g % HALF == 0:
                for s in range(HALF):
                    fetch(c + 1 + s, (nxt + s) % UNROLL).wait()
                part = g // HALF
                pair = t * (UNROLL // HALF) + part
                post(pair - 1, 1 - part)
                finish(pair - 2, part)
            for p in range(C // PIECE):
                for k in range(p * PIECE * K // C, (p + 1) * PIECE * K // C):
                    gather(slots[nxt], bufs[(g + 1) % 2], k)
                piece(bufs[g % 2], node, p * PIECE, g * C)
            if g % HALF == HALF - 1:
                for s in range(HALF):
                    n = c + 1 + UNROLL - HALF + 1 + s
                    fetch(n, (nxt - HALF + 1 + s) % UNROLL).start()
        return carry

    lax.fori_loop(0, nc // UNROLL, body, 0)
    pairs = nc // HALF
    post(pairs - 1, 1)
    finish(pairs - 2, 0)
    finish(pairs - 1, 1)
    for s in range(UNROLL):
        fetch(0, s).wait()


PAIR = HALF * C


def level1_kernel(
    base_ref, nbr, mask, owner, h1, prev, nxt, a1, b1, m1, u1, a_up, m_up, h1a, part, send_lo, send_hi,
    ext, tab, dst, idx_vm, s0, s1, s2, s3, r0, r1, z, msg, mc, mu, ma, mupc, fsem, csem
):
    nodes = h1a.shape[0]
    rows = ext.shape[0]
    loads = [(h1, REACH1, nodes), (prev, 0, REACH1), (nxt, REACH1 + nodes, REACH1)]
    copies = [
        pltpu.make_async_copy(src, ext.at[pl.ds(at, n), :], csem.at[i])
        for i, (src, at, n) in enumerate(loads)
    ]
    for cp in copies:
        cp.start()

    lane = lax.broadcasted_iota(jnp.int32, (K, L), 1)
    for c in range(nodes // C):
        cols = slice(c * C, (c + 1) * C)
        row = nbr[:, cols] + (lane + (REACH1 + c * C))
        idx_vm[c] = 2 * jnp.where(mask[:, cols] > 0, row, rows)
    mcv = centered(m1)
    mc[...] = mcv
    mu[...] = mm(mcv, u1[...]).astype(BF16)
    ma[...] = half(a_up)
    mupc[...] = centered(m_up)
    part[...] = jnp.zeros(part.shape, F32)
    msg[...] = jnp.zeros(msg.shape, BF16)
    for cp in copies:
        cp.wait()
    build_table(tab, ext, half(a1), rows)
    build_dst(dst, ext, REACH1, half(b1), nodes)

    def post(step, at):
        node = pl.multiple_of(jnp.maximum(step, 0) * PAIR, PAIR)
        hrow = ext[pl.ds(node + REACH1, PAIR), :].astype(F32)
        hb = (hrow + mm(z[pl.ds(at * PAIR, PAIR), :], mu[...])).astype(BF16)
        h1a[pl.ds(node, PAIR), :] = hb
        y = mm(act_of(mm(hb, ma[...])).astype(BF16), mupc[...])
        w = scale_of(y)
        msg[pl.ds(at * PAIR, PAIR), :] = jnp.concatenate(
            [y[:, :L] * w, y[:, L:] * w], axis=1
        ).astype(BF16)

    win = PAIR // 4 + 2 * REACH2

    def finish(step, at):
        live = jnp.where(step >= 0, 1.0, 0.0).astype(F32)
        pair = jnp.maximum(step, 0)
        first = pair * (PAIR // 4)
        ids = lax.broadcasted_iota(jnp.int32, (win, L), 0) + (base_ref[0] + first - REACH2)
        hot = []
        for j in range(HALF):
            ow = owner[pl.ds(pair * HALF + j, 1), :]
            hot.append(jnp.where(ids == ow, live, 0.0).astype(BF16))
        spot = pl.multiple_of(first, PAIR // 4)
        part[pl.ds(spot, win), :] += mm(
            jnp.concatenate(hot, axis=1), msg[pl.ds(at * PAIR, PAIR), :]
        )

    edge_loop(
        nodes // C, idx_vm, (s0, s1, s2, s3), fsem, (r0, r1), tab, dst, mc, z, post, finish
    )
    n = 2 * REACH2
    send_lo[...] = part[pl.ds(0, n), :].astype(BF16)
    send_hi[...] = part[pl.ds(part.shape[0] - n, n), :].astype(BF16)


def vmem():
    return pl.BlockSpec(memory_space=pltpu.VMEM)


def anyspace():
    return pl.BlockSpec(memory_space=pl.ANY)


def gather_scratch(rows, nodes):
    return [
        pltpu.VMEM((2 * rows + 8, L), F32),
        pltpu.VMEM((nodes, W), F32),
        pltpu.VMEM((nodes // C, K, L), jnp.int32),
        *[pltpu.SMEM((K, L), jnp.int32) for _ in range(UNROLL)],
        *[pltpu.VMEM((2 * K * C, L), F32) for _ in range(2)],
        pltpu.VMEM((UNROLL * C, W), BF16),
    ]


def level1(base, nbr_t, mask_t, owner2, h1, prev, nxt, weights):
    nodes = h1.shape[0]
    rows = nodes + 2 * REACH1
    n2 = nodes // 4
    edges = nodes * K
    shape = jax.ShapeDtypeStruct
    return pl.pallas_call(
        level1_kernel,
        out_shape=[
            shape((nodes, W), BF16),
            shape((n2 + 2 * REACH2, W), F32),
            shape((2 * REACH2, W), BF16),
            shape((2 * REACH2, W), BF16),
        ],
        in_specs=[pl.BlockSpec(memory_space=pltpu.SMEM)]
        + [vmem()] * 3
        + [anyspace()] * 3
        + [vmem()] * len(weights),
        out_specs=[vmem()] * 4,
        scratch_shapes=[
            pltpu.VMEM((rows, W), BF16),
            *gather_scratch(rows, nodes),
            pltpu.VMEM((UNROLL * C, W), BF16),
            *[pltpu.VMEM((W, W), BF16) for _ in range(4)],
            pltpu.SemaphoreType.DMA((UNROLL,)),
            pltpu.SemaphoreType.DMA((3,)),
        ],
        compiler_params=pltpu.CompilerParams(vmem_limit_bytes=VMEM_BYTES),
        cost_estimate=pl.CostEstimate(
            flops=4 * edges * W * W, bytes_accessed=rows * W * 4, transcendentals=edges * W
        ),
        name="level1",
    )(base, nbr_t, mask_t, owner2, h1, prev, nxt, *weights)


def level2_kernel(
    base_ref, nbr, mask, part, from_lo, from_hi, h2, lo2, hi2, u2, a2, b2, m2, v2, h2o, edge_lo, edge_hi,
    h2x, tab, dst, idx_vm, s0, s1, s2, s3, r0, r1, z, mc, mv, fsem
):
    n2 = h2o.shape[0]
    rows = n2 + 2 * REACH2
    S = 2 * REACH2
    u = u2[...]
    for q in range(rows // S):
        piece = part[pl.ds(q * S, S), :]
        if q == 0:
            piece = piece + from_lo[...].astype(F32)
        elif q == rows // S - 1:
            piece = piece + from_hi[...].astype(F32)
        d = mm(piece.astype(BF16), u)
        for hf in range(2):
            at = q * S + hf * REACH2
            if at == 0:
                src = lo2[...]
            elif at == rows - REACH2:
                src = hi2[...]
            else:
                src = h2[pl.ds(at - REACH2, REACH2), :]
            dd = d[hf * REACH2 : (hf + 1) * REACH2]
            h2x[pl.ds(at, REACH2), :] = (src.astype(F32) + dd).astype(BF16)
    lane = lax.broadcasted_iota(jnp.int32, (K, L), 1)
    base = base_ref[0]
    for c in range(n2 // C):
        cols = slice(c * C, (c + 1) * C)
        row = nbr[:, cols] - (base - REACH2)
        idx_vm[c] = 2 * jnp.where(mask[:, cols] > 0, row, rows)
    mcv = centered(m2)
    mc[...] = mcv
    mv[...] = mm(mcv, v2[...]).astype(BF16)
    build_table(tab, h2x, half(a2), rows)
    build_dst(dst, h2x, REACH2, half(b2), n2)

    def post(step, at):
        node = pl.multiple_of(jnp.maximum(step, 0) * PAIR, PAIR)
        hrow = h2x[pl.ds(node + REACH2, PAIR), :].astype(F32)
        h2o[pl.ds(node, PAIR), :] = (hrow + mm(z[pl.ds(at * PAIR, PAIR), :], mv[...])).astype(BF16)

    edge_loop(
        n2 // C, idx_vm, (s0, s1, s2, s3), fsem, (r0, r1), tab, dst, mc, z, post, lambda p, at: None
    )
    edge_lo[...] = h2o[pl.ds(0, REACH2), :]
    edge_hi[...] = h2o[pl.ds(n2 - REACH2, REACH2), :]


def level2(base, nbr_t, mask_t, part, from_lo, from_hi, h2, lo2, hi2, weights):
    nodes = h2.shape[0]
    rows = nodes + 2 * REACH2
    args = (base, nbr_t, mask_t, part, from_lo, from_hi, h2, lo2, hi2, *weights)
    shape = jax.ShapeDtypeStruct
    return pl.pallas_call(
        level2_kernel,
        out_shape=[shape((nodes, W), BF16), shape((REACH2, W), BF16), shape((REACH2, W), BF16)],
        in_specs=[pl.BlockSpec(memory_space=pltpu.SMEM)] + [vmem()] * (len(args) - 1),
        out_specs=[vmem()] * 3,
        scratch_shapes=[
            pltpu.VMEM((rows, W), BF16),
            *gather_scratch(rows, nodes),
            pltpu.VMEM((W, W), BF16),
            pltpu.VMEM((W, W), BF16),
            pltpu.SemaphoreType.DMA((UNROLL,)),
        ],
        compiler_params=pltpu.CompilerParams(vmem_limit_bytes=VMEM_BYTES),
        cost_estimate=pl.CostEstimate(
            flops=4 * nodes * K * W * W, bytes_accessed=rows * W * 4, transcendentals=nodes * K * W
        ),
        name="level2",
    )(*args)


DOWN = 2048
GROUP = 512


def down_kernel(base_ref, owner, h1a, h2o, lo, hi, a_down, b_down, m_down, o_ref, pd, bd, mdc):
    t = pl.program_id(0)
    n2 = h2o.shape[0]

    @pl.when(t == 0)
    def _():
        a = half(a_down)
        pd[pl.ds(0, REACH2), :] = mm(lo[...], a).astype(BF16)
        for b in range(n2 // 256):
            pd[pl.ds(REACH2 + b * 256, 256), :] = mm(h2o[pl.ds(b * 256, 256), :], a).astype(BF16)
        pd[pl.ds(REACH2 + n2, REACH2), :] = mm(hi[...], a).astype(BF16)
        bd[...] = half(b_down)
        mdc[...] = centered(m_down)

    win = GROUP // 4 + 2 * REACH2
    lane = lax.broadcasted_iota(jnp.int32, (L, L), 1).astype(F32)
    for g in range(DOWN // GROUP):
        start = t * (DOWN // 4) + g * (GROUP // 4)
        lowest = base_ref[0] + start - REACH2
        table = pd[pl.ds(pl.multiple_of(start, L), win), :]
        hot = []
        for j in range(GROUP // L):
            ow = owner[pl.ds(t * (DOWN // L) + g * (GROUP // L) + j, 1), :] - lowest
            col = jnp.transpose(jnp.broadcast_to(ow.astype(F32), (L, L)))
            hot.append(
                jnp.concatenate(
                    [jnp.where(col == lane + q * L, 1.0, 0.0).astype(BF16) for q in range(win // L)],
                    axis=1,
                )
            )
        hb = h1a[pl.ds(g * GROUP, GROUP), :]
        y = mm(jnp.concatenate(hot, axis=0), table) + mm(hb, bd[...])
        d = mm(act_of(y).astype(BF16), mdc[...])
        w = scale_of(d)
        ln = jnp.concatenate([d[:, :L] * w, d[:, L:] * w], axis=1)
        o_ref[pl.ds(g * GROUP, GROUP), :] = (hb.astype(F32) + ln).astype(BF16)


def down(base, owner2, h1a, h2o, lo, hi, a_down, b_down, m_down):
    nodes1 = h1a.shape[0]
    n2 = h2o.shape[0]

    def whole(shape):
        return pl.BlockSpec(shape, lambda t: (0, 0))

    block = pl.BlockSpec((DOWN, W), lambda t: (t, 0))
    return pl.pallas_call(
        down_kernel,
        grid=(nodes1 // DOWN,),
        out_shape=jax.ShapeDtypeStruct((nodes1, W), BF16),
        in_specs=[
            pl.BlockSpec(memory_space=pltpu.SMEM),
            whole(owner2.shape),
            block,
            whole((n2, W)),
            whole((REACH2, W)),
            whole((REACH2, W)),
            whole((W, W)),
            whole((W, W)),
            whole((W, W)),
        ],
        out_specs=block,
        scratch_shapes=[
            pltpu.VMEM((n2 + 2 * REACH2, W), BF16),
            pltpu.VMEM((W, W), BF16),
            pltpu.VMEM((W, W), BF16),
        ],
        compiler_params=pltpu.CompilerParams(vmem_limit_bytes=VMEM_BYTES),
        cost_estimate=pl.CostEstimate(
            flops=10 * nodes1 * W * W, bytes_accessed=nodes1 * W * 4, transcendentals=nodes1 * W
        ),
        name="down",
    )(base, owner2, h1a, h2o, lo, hi, a_down, b_down, m_down)


def swap(to_next, to_prev, axis):
    count = lax.axis_size(axis)
    ends = count - 1
    from_prev = lax.ppermute(to_next, axis, [(i, (i + 1) % count) for i in range(ends)])
    from_next = lax.ppermute(to_prev, axis, [((i + 1) % count, i) for i in range(ends)])
    return from_prev, from_next


def shards(
    h1,
    h2,
    nbr1,
    mask1,
    owner,
    nbr2,
    mask2,
    a1,
    b1,
    m1,
    u1,
    a_up,
    m_up,
    u2,
    a2,
    b2,
    m2,
    v2,
    a_down,
    b_down,
    m_down,
):
    nodes1 = h1.shape[0]
    nodes2 = h2.shape[0]
    device = lax.axis_index("grp") * lax.axis_size("sub") + lax.axis_index("sub")
    base = jnp.reshape(device * nodes2, (1,)).astype(jnp.int32)
    nbr1_t, mask1_t, nbr2_t, mask2_t = nbr1.T, mask1.T, nbr2.T, mask2.T
    owner2 = owner.reshape(nodes1 // L, L)
    halo1 = swap(h1[nodes1 - REACH1 :], h1[:REACH1], ("grp", "sub"))
    halo2 = swap(h2[nodes2 - REACH2 :], h2[:REACH2], "sub")
    h1a, part, send_lo, send_hi = level1(
        base, nbr1_t, mask1_t, owner2, h1, *halo1, (a1, b1, m1, u1, a_up, m_up)
    )
    from_lo, from_hi = swap(send_hi, send_lo, "sub")
    h2_out, edge_lo, edge_hi = level2(
        base, nbr2_t, mask2_t, part, from_lo, from_hi, h2, *halo2, (u2, a2, b2, m2, v2)
    )
    lo, hi = swap(edge_hi, edge_lo, "sub")
    h1_out = down(base, owner2, h1a, h2_out, lo, hi, a_down, b_down, m_down)
    return (h1_out, h2_out)


def solution(mesh):
    split = P(("grp", "sub"), None)
    return jax.shard_map(
        shards,
        mesh=mesh,
        in_specs=(split, split, split, split, P(("grp", "sub")), split, split) + (P(),) * 14,
        out_specs=(split, split),
        check_vma=False,
    )
```

```python
import functools

import jax
import jax.numpy as jnp
from jax import lax
from jax.experimental import pallas as pl
from jax.experimental.pallas import tpu as pltpu
from jax.sharding import PartitionSpec as P

F32 = jnp.float32
BF16 = jnp.bfloat16
W = 256
L = 128
K = 8
C = 128
UNROLL = 4
HALF = 2
PAIR = HALF * C
PIECE = 32
DEAD = -10000.0
EPS = 1e-05
VMEM_BYTES = 56 * 2**20
REACH1 = 1024
REACH2 = 256


def mm(x, y):
    return jnp.dot(x, y, preferred_element_type=F32)


def half(ref):
    return (ref[...].astype(F32) * 0.5).astype(BF16)


def centered(ref):
    w = ref[...].astype(F32)
    return (w - jnp.mean(w, axis=1, keepdims=True)).astype(BF16)


def act_of(y):
    return y + y * jnp.tanh(y)


def ones_block():
    return jnp.full((L, L), 1.0 / W, BF16)


def scale_of(y):
    lo = y[:, :L]
    hi = y[:, L:]
    s = jnp.sum(lo * lo + hi * hi, axis=1, keepdims=True)
    return lax.rsqrt(s * (1.0 / W) + EPS)


def store_table(tab, row0, p):
    n = p.shape[0]
    tab[pl.ds(2 * row0, n, stride=2), :] = p[:, :L]
    tab[pl.ds(2 * row0 + 1, n, stride=2), :] = p[:, L:]


def build_table(tab, ext, a, row0, rows):
    step = 1024 if rows % 1024 == 0 else 512

    def one(b, carry):
        r = pl.multiple_of(row0 + b * step, step)
        store_table(tab, r, mm(ext[pl.ds(r, step), :], a))
        return carry

    lax.fori_loop(0, rows // step, one, 0)


def edge_loop(nc, idx_vm, slots, sems, bufs, tab, dst, mc, z, receivers, post, finish):
    def fetch(c, s):
        return pltpu.make_async_copy(idx_vm.at[jnp.minimum(c, nc - 1)], slots[s], sems.at[s])

    def gather(slot, buf, k):
        for i in range(C):
            j = slot[k, i]
            buf[pl.ds(2 * (k * C + i), 2), :] = tab[pl.ds(j, 2), :]

    def piece(buf, i0, zrow):
        d = dst[pl.ds(zrow + i0, PIECE), :]
        d0 = d[:, :L]
        d1 = d[:, L:]
        acts = []
        for k in range(K):
            base = 2 * (k * C + i0)
            y0 = buf[pl.ds(base, PIECE, stride=2), :] + d0
            y1 = buf[pl.ds(base + 1, PIECE, stride=2), :] + d1
            acts.append(jnp.concatenate([act_of(y0), act_of(y1)], axis=1).astype(BF16))
        y = mm(jnp.concatenate(acts, axis=0), mc[...])
        lo = y[:, :L]
        hi = y[:, L:]
        w = lax.rsqrt(jnp.sum(lo * lo + hi * hi, axis=1, keepdims=True) + EPS)
        acc0 = acc1 = None
        for k in range(K):
            wk = w[k * PIECE : (k + 1) * PIECE]
            a = acts[k].astype(F32)
            t0 = a[:, :L] * wk
            t1 = a[:, L:] * wk
            acc0 = t0 if k == 0 else acc0 + t0
            acc1 = t1 if k == 0 else acc1 + t1
        z[pl.ds(zrow + i0, PIECE), :] = jnp.concatenate([acc0, acc1], axis=1).astype(BF16)

    z[...] = jnp.zeros(z.shape, BF16)
    dst[pl.ds(0, PAIR), :] = receivers(0)
    for s in range(UNROLL):
        fetch(s, s).start()
    fetch(0, 0).wait()
    for k in range(K):
        gather(slots[0], bufs[0], k)
    fetch(UNROLL, 0).start()

    def body(t, carry):
        for g in range(UNROLL):
            c = t * UNROLL + g
            nxt = (g + 1) % UNROLL
            if g % HALF == 0:
                for s in range(HALF):
                    fetch(c + 1 + s, (nxt + s) % UNROLL).wait()
                part = g // HALF
                pair = t * (UNROLL // HALF) + part
                dst[pl.ds((1 - part) * PAIR, PAIR), :] = receivers(jnp.minimum(pair + 1, nc // HALF - 1))
                post(pair - 1, 1 - part)
                finish(pair - 2, part)
            for p in range(C // PIECE):
                for k in range(p * PIECE * K // C, (p + 1) * PIECE * K // C):
                    gather(slots[nxt], bufs[(g + 1) % 2], k)
                piece(bufs[g % 2], p * PIECE, g * C)
            if g % HALF == HALF - 1:
                for s in range(HALF):
                    n = c + 1 + UNROLL - HALF + 1 + s
                    fetch(n, (nxt - HALF + 1 + s) % UNROLL).start()
        return carry

    lax.fori_loop(0, nc // UNROLL, body, 0)
    pairs = nc // HALF
    post(pairs - 1, 1)
    finish(pairs - 2, 0)
    finish(pairs - 1, 1)
    for s in range(UNROLL):
        fetch(0, s).wait()


def level1_kernel(
    base_ref, nbr, mask, owner, h1, prev, nxt, a1, b1, m1, u1, a_up, m_up, h1a, part, send_lo, send_hi,
    ext, tab, dst, idx_vm, s0, s1, s2, s3, r0, r1, z, msg, mc, mu, ma, mupc, bh, fsem, csem
):
    nodes = h1a.shape[0]
    rows = ext.shape[0]
    cut = nodes // 4
    loads = [(h1, q * cut, REACH1 + q * cut, cut) for q in range(4)]
    loads += [(prev, 0, 0, REACH1), (nxt, 0, REACH1 + nodes, REACH1)]
    copies = [
        pltpu.make_async_copy(src.at[pl.ds(off, n), :], ext.at[pl.ds(at, n), :], csem.at[i])
        for i, (src, off, at, n) in enumerate(loads)
    ]
    for cp in copies:
        cp.start()

    lane = lax.broadcasted_iota(jnp.int32, (K, L), 1)
    for c in range(nodes // C):
        cols = slice(c * C, (c + 1) * C)
        row = nbr[:, cols] + (lane + (REACH1 + c * C))
        idx_vm[c] = 2 * jnp.where(mask[:, cols] > 0, row, rows)
    mcv = centered(m1)
    mc[...] = mcv * (1.0 / 16.0)
    mu[...] = mm(mcv, u1[...]).astype(BF16)
    ma[...] = half(a_up)
    mupc[...] = centered(m_up)
    part[...] = jnp.zeros(part.shape, F32)
    msg[...] = jnp.zeros(msg.shape, BF16)
    ah = half(a1)
    bh[...] = half(b1)
    for cp, (_, _, at, n) in zip(copies, loads):
        cp.wait()
        build_table(tab, ext, ah, at, n)
    tab[pl.ds(2 * rows, 8), :] = jnp.full((8, L), DEAD, F32)

    def receivers(pair):
        return mm(ext[pl.ds(pl.multiple_of(pair * PAIR, PAIR) + REACH1, PAIR), :], bh[...])

    def post(step, at):
        node = pl.multiple_of(jnp.maximum(step, 0) * PAIR, PAIR)
        hrow = ext[pl.ds(node + REACH1, PAIR), :].astype(F32)
        hb = (hrow + mm(z[pl.ds(at * PAIR, PAIR), :], mu[...])).astype(BF16)
        h1a[pl.ds(node, PAIR), :] = hb
        y = mm(act_of(mm(hb, ma[...])).astype(BF16), mupc[...])
        w = scale_of(y)
        msg[pl.ds(at * PAIR, PAIR), :] = jnp.concatenate(
            [y[:, :L] * w, y[:, L:] * w], axis=1
        ).astype(BF16)

    win = PAIR // 4 + 2 * REACH2

    def finish(step, at):
        live = jnp.where(step >= 0, 1.0, 0.0).astype(F32)
        pair = jnp.maximum(step, 0)
        first = pair * (PAIR // 4)
        ids = lax.broadcasted_iota(jnp.int32, (win, L), 0) + (base_ref[0] + first - REACH2)
        hot = []
        for j in range(HALF):
            ow = owner[pl.ds(pair * HALF + j, 1), :]
            hot.append(jnp.where(ids == ow, live, 0.0).astype(BF16))
        spot = pl.multiple_of(first, PAIR // 4)
        part[pl.ds(spot, win), :] += mm(
            jnp.concatenate(hot, axis=1), msg[pl.ds(at * PAIR, PAIR), :]
        )

    edge_loop(
        nodes // C, idx_vm, (s0, s1, s2, s3), fsem, (r0, r1), tab, dst, mc, z, receivers, post, finish
    )
    n = 2 * REACH2
    send_lo[...] = part[pl.ds(0, n), :].astype(BF16)
    send_hi[...] = part[pl.ds(part.shape[0] - n, n), :].astype(BF16)


def vmem():
    return pl.BlockSpec(memory_space=pltpu.VMEM)


def anyspace():
    return pl.BlockSpec(memory_space=pl.ANY)


def gather_scratch(rows, nodes):
    return [
        pltpu.VMEM((2 * rows + 8, L), F32),
        pltpu.VMEM((2 * PAIR, W), F32),
        pltpu.VMEM((nodes // C, K, L), jnp.int32),
        *[pltpu.SMEM((K, L), jnp.int32) for _ in range(UNROLL)],
        *[pltpu.VMEM((2 * K * C, L), F32) for _ in range(2)],
        pltpu.VMEM((UNROLL * C, W), BF16),
    ]


def level1(base, nbr_t, mask_t, owner2, h1, prev, nxt, weights):
    nodes = h1.shape[0]
    rows = nodes + 2 * REACH1
    n2 = nodes // 4
    edges = nodes * K
    shape = jax.ShapeDtypeStruct
    return pl.pallas_call(
        level1_kernel,
        out_shape=[
            shape((nodes, W), BF16),
            shape((n2 + 2 * REACH2, W), F32),
            shape((2 * REACH2, W), BF16),
            shape((2 * REACH2, W), BF16),
        ],
        in_specs=[pl.BlockSpec(memory_space=pltpu.SMEM)]
        + [vmem()] * 3
        + [anyspace()] * 3
        + [vmem()] * len(weights),
        out_specs=[vmem()] * 4,
        scratch_shapes=[
            pltpu.VMEM((rows, W), BF16),
            *gather_scratch(rows, nodes),
            pltpu.VMEM((UNROLL * C, W), BF16),
            *[pltpu.VMEM((W, W), BF16) for _ in range(5)],
            pltpu.SemaphoreType.DMA((UNROLL,)),
            pltpu.SemaphoreType.DMA((6,)),
        ],
        compiler_params=pltpu.CompilerParams(vmem_limit_bytes=VMEM_BYTES),
        cost_estimate=pl.CostEstimate(
            flops=4 * edges * W * W, bytes_accessed=rows * W * 4, transcendentals=edges * W
        ),
        name="level1",
    )(base, nbr_t, mask_t, owner2, h1, prev, nxt, *weights)


def level2_kernel(
    base_ref, nbr, mask, part, from_lo, from_hi, h2, lo2, hi2, u2, a2, b2, m2, v2, h2o, edge_lo, edge_hi,
    h2x, tab, dst, idx_vm, s0, s1, s2, s3, r0, r1, z, mc, mv, bh, fsem
):
    n2 = h2o.shape[0]
    rows = n2 + 2 * REACH2
    S = 2 * REACH2
    u = u2[...]
    for q in range(rows // S):
        piece = part[pl.ds(q * S, S), :]
        if q == 0:
            piece = piece + from_lo[...].astype(F32)
        elif q == rows // S - 1:
            piece = piece + from_hi[...].astype(F32)
        d = mm(piece.astype(BF16), u)
        for hf in range(2):
            at = q * S + hf * REACH2
            if at == 0:
                src = lo2[...]
            elif at == rows - REACH2:
                src = hi2[...]
            else:
                src = h2[pl.ds(at - REACH2, REACH2), :]
            dd = d[hf * REACH2 : (hf + 1) * REACH2]
            h2x[pl.ds(at, REACH2), :] = (src.astype(F32) + dd).astype(BF16)
    lane = lax.broadcasted_iota(jnp.int32, (K, L), 1)
    base = base_ref[0]
    for c in range(n2 // C):
        cols = slice(c * C, (c + 1) * C)
        row = nbr[:, cols] - (base - REACH2)
        idx_vm[c] = 2 * jnp.where(mask[:, cols] > 0, row, rows)
    mcv = centered(m2)
    mc[...] = mcv * (1.0 / 16.0)
    mv[...] = mm(mcv, v2[...]).astype(BF16)
    build_table(tab, h2x, half(a2), 0, rows)
    tab[pl.ds(2 * rows, 8), :] = jnp.full((8, L), DEAD, F32)
    bh[...] = half(b2)

    def receivers(pair):
        return mm(h2x[pl.ds(pl.multiple_of(pair * PAIR, PAIR) + REACH2, PAIR), :], bh[...])

    def post(step, at):
        node = pl.multiple_of(jnp.maximum(step, 0) * PAIR, PAIR)
        hrow = h2x[pl.ds(node + REACH2, PAIR), :].astype(F32)
        h2o[pl.ds(node, PAIR), :] = (hrow + mm(z[pl.ds(at * PAIR, PAIR), :], mv[...])).astype(BF16)

    edge_loop(
        n2 // C, idx_vm, (s0, s1, s2, s3), fsem, (r0, r1), tab, dst, mc, z, receivers, post, lambda p, at: None
    )
    edge_lo[...] = h2o[pl.ds(0, REACH2), :]
    edge_hi[...] = h2o[pl.ds(n2 - REACH2, REACH2), :]


def level2(base, nbr_t, mask_t, part, from_lo, from_hi, h2, lo2, hi2, weights):
    nodes = h2.shape[0]
    rows = nodes + 2 * REACH2
    args = (base, nbr_t, mask_t, part, from_lo, from_hi, h2, lo2, hi2, *weights)
    shape = jax.ShapeDtypeStruct
    return pl.pallas_call(
        level2_kernel,
        out_shape=[shape((nodes, W), BF16), shape((REACH2, W), BF16), shape((REACH2, W), BF16)],
        grid=(1,),
        in_specs=[pl.BlockSpec(memory_space=pltpu.SMEM)]
        + [vmem()] * 6
        + [pl.BlockSpec((REACH2, W), lambda t: (REACH1 // REACH2, 0))] * 2
        + [vmem()] * len(weights),
        out_specs=[vmem()] * 3,
        scratch_shapes=[
            pltpu.VMEM((rows, W), BF16),
            *gather_scratch(rows, nodes),
            *[pltpu.VMEM((W, W), BF16) for _ in range(3)],
            pltpu.SemaphoreType.DMA((UNROLL,)),
        ],
        compiler_params=pltpu.CompilerParams(vmem_limit_bytes=VMEM_BYTES),
        cost_estimate=pl.CostEstimate(
            flops=4 * nodes * K * W * W, bytes_accessed=rows * W * 4, transcendentals=nodes * K * W
        ),
        name="level2",
    )(*args)


DOWN = 2048
GROUP = 512


def down_kernel(base_ref, owner, h1a, h2o, lo, hi, a_down, b_down, m_down, o_ref, pd, bd, mdc):
    t = pl.program_id(0)
    n2 = h2o.shape[0]

    @pl.when(t == 0)
    def _():
        a = half(a_down)
        pd[pl.ds(0, REACH2), :] = mm(lo[...], a).astype(BF16)
        for b in range(n2 // 256):
            pd[pl.ds(REACH2 + b * 256, 256), :] = mm(h2o[pl.ds(b * 256, 256), :], a).astype(BF16)
        pd[pl.ds(REACH2 + n2, REACH2), :] = mm(hi[...], a).astype(BF16)
        bd[...] = half(b_down)
        mdc[...] = centered(m_down)

    win = GROUP // 4 + 2 * REACH2
    lane = lax.broadcasted_iota(jnp.int32, (L, L), 1).astype(F32)
    for g in range(DOWN // GROUP):
        start = t * (DOWN // 4) + g * (GROUP // 4)
        lowest = base_ref[0] + start - REACH2
        table = pd[pl.ds(pl.multiple_of(start, L), win), :]
        hot = []
        for j in range(GROUP // L):
            ow = owner[pl.ds(t * (DOWN // L) + g * (GROUP // L) + j, 1), :] - lowest
            col = jnp.transpose(jnp.broadcast_to(ow.astype(F32), (L, L)))
            hot.append(
                jnp.concatenate(
                    [jnp.where(col == lane + q * L, 1.0, 0.0).astype(BF16) for q in range(win // L)],
                    axis=1,
                )
            )
        hb = h1a[pl.ds(g * GROUP, GROUP), :]
        y = mm(jnp.concatenate(hot, axis=0), table) + mm(hb, bd[...])
        d = mm(act_of(y).astype(BF16), mdc[...])
        w = scale_of(d)
        ln = jnp.concatenate([d[:, :L] * w, d[:, L:] * w], axis=1)
        o_ref[pl.ds(g * GROUP, GROUP), :] = (hb.astype(F32) + ln).astype(BF16)


def down(base, owner2, h1a, h2o, lo, hi, a_down, b_down, m_down):
    nodes1 = h1a.shape[0]
    n2 = h2o.shape[0]

    def whole(shape):
        return pl.BlockSpec(shape, lambda t: (0, 0))

    block = pl.BlockSpec((DOWN, W), lambda t: (t, 0))
    return pl.pallas_call(
        down_kernel,
        grid=(nodes1 // DOWN,),
        out_shape=jax.ShapeDtypeStruct((nodes1, W), BF16),
        in_specs=[
            pl.BlockSpec(memory_space=pltpu.SMEM),
            whole(owner2.shape),
            block,
            whole((n2, W)),
            whole((REACH2, W)),
            whole((REACH2, W)),
            whole((W, W)),
            whole((W, W)),
            whole((W, W)),
        ],
        out_specs=block,
        scratch_shapes=[
            pltpu.VMEM((n2 + 2 * REACH2, W), BF16),
            pltpu.VMEM((W, W), BF16),
            pltpu.VMEM((W, W), BF16),
        ],
        compiler_params=pltpu.CompilerParams(vmem_limit_bytes=VMEM_BYTES),
        cost_estimate=pl.CostEstimate(
            flops=10 * nodes1 * W * W, bytes_accessed=nodes1 * W * 4, transcendentals=nodes1 * W
        ),
        name="down",
    )(base, owner2, h1a, h2o, lo, hi, a_down, b_down, m_down)


def swap(to_next, to_prev, axis):
    count = lax.axis_size(axis)
    ends = count - 1
    from_prev = lax.ppermute(to_next, axis, [(i, (i + 1) % count) for i in range(ends)])
    from_next = lax.ppermute(to_prev, axis, [((i + 1) % count, i) for i in range(ends)])
    return from_prev, from_next


def shards(
    h1,
    h2,
    nbr1,
    mask1,
    owner,
    nbr2,
    mask2,
    a1,
    b1,
    m1,
    u1,
    a_up,
    m_up,
    u2,
    a2,
    b2,
    m2,
    v2,
    a_down,
    b_down,
    m_down,
):
    nodes1 = h1.shape[0]
    nodes2 = h2.shape[0]
    device = lax.axis_index("grp") * lax.axis_size("sub") + lax.axis_index("sub")
    base = jnp.reshape(device * nodes2, (1,)).astype(jnp.int32)
    nbr1_t, mask1_t, nbr2_t, mask2_t = nbr1.T, mask1.T, nbr2.T, mask2.T
    owner2 = owner.reshape(nodes1 // L, L)
    halo = swap(
        jnp.concatenate([h1[nodes1 - REACH1 :], h2[nodes2 - REACH2 :]], axis=0),
        jnp.concatenate([h1[:REACH1], h2[:REACH2]], axis=0),
        ("grp", "sub"),
    )
    h1a, part, send_lo, send_hi = level1(
        base, nbr1_t, mask1_t, owner2, h1, *halo, (a1, b1, m1, u1, a_up, m_up)
    )
    from_lo, from_hi = swap(send_hi, send_lo, "sub")
    h2_out, edge_lo, edge_hi = level2(
        base, nbr2_t, mask2_t, part, from_lo, from_hi, h2, *halo, (u2, a2, b2, m2, v2)
    )
    lo, hi = swap(edge_hi, edge_lo, "sub")
    h1_out = down(base, owner2, h1a, h2_out, lo, hi, a_down, b_down, m_down)
    return (h1_out, h2_out)


def solution(mesh):
    split = P(("grp", "sub"), None)
    return jax.shard_map(
        shards,
        mesh=mesh,
        in_specs=(split, split, split, split, P(("grp", "sub")), split, split) + (P(),) * 14,
        out_specs=(split, split),
        check_vma=False,
    )
```

```python
import functools

import jax
import jax.numpy as jnp
from jax import lax
from jax.experimental import pallas as pl
from jax.experimental.pallas import tpu as pltpu
from jax.sharding import PartitionSpec as P

F32 = jnp.float32
BF16 = jnp.bfloat16
W = 256
L = 128
K = 8
C = 128
UNROLL = 4
HALF = 2
PAIR = HALF * C
PIECE = 32
DEAD = -10000.0
EPS = 1e-05
VMEM_BYTES = 56 * 2**20
REACH1 = 1024
REACH2 = 256


def mm(x, y):
    return jnp.dot(x, y, preferred_element_type=F32)


def half(ref):
    return (ref[...].astype(F32) * 0.5).astype(BF16)


def centered(ref):
    w = ref[...].astype(F32)
    return (w - jnp.mean(w, axis=1, keepdims=True)).astype(BF16)


def act_of(y):
    return y + y * jnp.tanh(y)


def is_odd(base_ref, n2):
    return lax.rem(lax.div(base_ref[0], n2), 2) == 1


def pick(odd, a, b):
    return jnp.where(odd, a.astype(F32), b.astype(F32))


def ones_block():
    return jnp.full((L, L), 1.0 / W, BF16)


def scale_of(y):
    lo = y[:, :L]
    hi = y[:, L:]
    s = jnp.sum(lo * lo + hi * hi, axis=1, keepdims=True)
    return lax.rsqrt(s * (1.0 / W) + EPS)


def store_table(tab, row0, p):
    n = p.shape[0]
    tab[pl.ds(2 * row0, n, stride=2), :] = p[:, :L]
    tab[pl.ds(2 * row0 + 1, n, stride=2), :] = p[:, L:]


def build_table(tab, ext, a, row0, rows):
    step = 1024 if rows % 1024 == 0 else 512

    def one(b, carry):
        r = pl.multiple_of(row0 + b * step, step)
        store_table(tab, r, mm(ext[pl.ds(r, step), :], a))
        return carry

    lax.fori_loop(0, rows // step, one, 0)


def edge_loop(nc, idx_vm, slots, sems, bufs, tab, dst, mc, z, receivers, post, finish):
    def fetch(c, s):
        return pltpu.make_async_copy(idx_vm.at[jnp.minimum(c, nc - 1)], slots[s], sems.at[s])

    def gather(slot, buf, k):
        for i in range(C):
            j = slot[k, i]
            buf[pl.ds(2 * (k * C + i), 2), :] = tab[pl.ds(j, 2), :]

    def piece(buf, i0, zrow):
        d = dst[pl.ds(zrow + i0, PIECE), :]
        d0 = d[:, :L]
        d1 = d[:, L:]
        acts = []
        for k in range(K):
            base = 2 * (k * C + i0)
            y0 = buf[pl.ds(base, PIECE, stride=2), :] + d0
            y1 = buf[pl.ds(base + 1, PIECE, stride=2), :] + d1
            acts.append(jnp.concatenate([act_of(y0), act_of(y1)], axis=1).astype(BF16))
        y = mm(jnp.concatenate(acts, axis=0), mc[...])
        lo = y[:, :L]
        hi = y[:, L:]
        w = lax.rsqrt(jnp.sum(lo * lo + hi * hi, axis=1, keepdims=True) + EPS)
        acc0 = acc1 = None
        for k in range(K):
            wk = w[k * PIECE : (k + 1) * PIECE]
            a = acts[k].astype(F32)
            t0 = a[:, :L] * wk
            t1 = a[:, L:] * wk
            acc0 = t0 if k == 0 else acc0 + t0
            acc1 = t1 if k == 0 else acc1 + t1
        z[pl.ds(zrow + i0, PIECE), :] = jnp.concatenate([acc0, acc1], axis=1).astype(BF16)

    z[...] = jnp.zeros(z.shape, BF16)
    dst[pl.ds(0, PAIR), :] = receivers(0)
    for s in range(UNROLL):
        fetch(s, s).start()
    fetch(0, 0).wait()
    for k in range(K):
        gather(slots[0], bufs[0], k)
    fetch(UNROLL, 0).start()

    def body(t, carry):
        for g in range(UNROLL):
            c = t * UNROLL + g
            nxt = (g + 1) % UNROLL
            if g % HALF == 0:
                for s in range(HALF):
                    fetch(c + 1 + s, (nxt + s) % UNROLL).wait()
                part = g // HALF
                pair = t * (UNROLL // HALF) + part
                dst[pl.ds((1 - part) * PAIR, PAIR), :] = receivers(jnp.minimum(pair + 1, nc // HALF - 1))
                post(pair - 1, 1 - part)
                finish(pair - 2, part)
            for p in range(C // PIECE):
                for k in range(p * PIECE * K // C, (p + 1) * PIECE * K // C):
                    gather(slots[nxt], bufs[(g + 1) % 2], k)
                piece(bufs[g % 2], p * PIECE, g * C)
            if g % HALF == HALF - 1:
                for s in range(HALF):
                    n = c + 1 + UNROLL - HALF + 1 + s
                    fetch(n, (nxt - HALF + 1 + s) % UNROLL).start()
        return carry

    lax.fori_loop(0, nc // UNROLL, body, 0)
    pairs = nc // HALF
    post(pairs - 1, 1)
    finish(pairs - 2, 0)
    finish(pairs - 1, 1)
    for s in range(UNROLL):
        fetch(0, s).wait()


def level1_kernel(
    base_ref, nbr, mask, owner, h1, near, far, a1, b1, m1, u1, a_up, m_up, h1a, part, inner, outer,
    ext, tab, dst, idx_vm, s0, s1, s2, s3, r0, r1, z, msg, mc, mu, ma, mupc, bh, fsem, csem
):
    nodes = h1a.shape[0]
    rows = ext.shape[0]
    cut = nodes // 4
    loads = [(h1, q * cut, REACH1 + q * cut, cut) for q in range(4)]
    odd = is_odd(base_ref, nodes // 4)
    near_at = pl.multiple_of(jnp.where(odd, 0, REACH1 + nodes), REACH1)
    far_at = pl.multiple_of(jnp.where(odd, REACH1 + nodes, 0), REACH1)
    loads += [(near, 0, near_at, REACH1), (far, 0, far_at, REACH1)]
    copies = [
        pltpu.make_async_copy(src.at[pl.ds(off, n), :], ext.at[pl.ds(at, n), :], csem.at[i])
        for i, (src, off, at, n) in enumerate(loads)
    ]
    for cp in copies:
        cp.start()

    lane = lax.broadcasted_iota(jnp.int32, (K, L), 1)
    for c in range(nodes // C):
        cols = slice(c * C, (c + 1) * C)
        row = nbr[:, cols] + (lane + (REACH1 + c * C))
        idx_vm[c] = 2 * jnp.where(mask[:, cols] > 0, row, rows)
    mcv = centered(m1)
    mc[...] = mcv * (1.0 / 16.0)
    mu[...] = mm(mcv, u1[...]).astype(BF16)
    ma[...] = half(a_up)
    mupc[...] = centered(m_up)
    part[...] = jnp.zeros(part.shape, F32)
    msg[...] = jnp.zeros(msg.shape, BF16)
    ah = half(a1)
    bh[...] = half(b1)
    for cp, (_, _, at, n) in zip(copies, loads):
        cp.wait()
        build_table(tab, ext, ah, at, n)
    tab[pl.ds(2 * rows, 8), :] = jnp.full((8, L), DEAD, F32)

    def receivers(pair):
        return mm(ext[pl.ds(pl.multiple_of(pair * PAIR, PAIR) + REACH1, PAIR), :], bh[...])

    def post(step, at):
        node = pl.multiple_of(jnp.maximum(step, 0) * PAIR, PAIR)
        hrow = ext[pl.ds(node + REACH1, PAIR), :].astype(F32)
        hb = (hrow + mm(z[pl.ds(at * PAIR, PAIR), :], mu[...])).astype(BF16)
        h1a[pl.ds(node, PAIR), :] = hb
        y = mm(act_of(mm(hb, ma[...])).astype(BF16), mupc[...])
        w = scale_of(y)
        msg[pl.ds(at * PAIR, PAIR), :] = jnp.concatenate(
            [y[:, :L] * w, y[:, L:] * w], axis=1
        ).astype(BF16)

    win = PAIR // 4 + 2 * REACH2

    def finish(step, at):
        live = jnp.where(step >= 0, 1.0, 0.0).astype(F32)
        pair = jnp.maximum(step, 0)
        first = pair * (PAIR // 4)
        ids = lax.broadcasted_iota(jnp.int32, (win, L), 0) + (base_ref[0] + first - REACH2)
        hot = []
        for j in range(HALF):
            ow = owner[pl.ds(pair * HALF + j, 1), :]
            hot.append(jnp.where(ids == ow, live, 0.0).astype(BF16))
        spot = pl.multiple_of(first, PAIR // 4)
        part[pl.ds(spot, win), :] += mm(
            jnp.concatenate(hot, axis=1), msg[pl.ds(at * PAIR, PAIR), :]
        )

    edge_loop(
        nodes // C, idx_vm, (s0, s1, s2, s3), fsem, (r0, r1), tab, dst, mc, z, receivers, post, finish
    )
    n = 2 * REACH2
    low = part[pl.ds(0, n), :]
    up = part[pl.ds(part.shape[0] - n, n), :]
    inner[...] = pick(odd, low, up).astype(BF16)
    outer[...] = pick(odd, up, low).astype(BF16)


def vmem():
    return pl.BlockSpec(memory_space=pltpu.VMEM)


def anyspace():
    return pl.BlockSpec(memory_space=pl.ANY)


def gather_scratch(rows, nodes):
    return [
        pltpu.VMEM((2 * rows + 8, L), F32),
        pltpu.VMEM((2 * PAIR, W), F32),
        pltpu.VMEM((nodes // C, K, L), jnp.int32),
        *[pltpu.SMEM((K, L), jnp.int32) for _ in range(UNROLL)],
        *[pltpu.VMEM((2 * K * C, L), F32) for _ in range(2)],
        pltpu.VMEM((UNROLL * C, W), BF16),
    ]


def level1(base, nbr_t, mask_t, owner2, h1, prev, nxt, weights):
    nodes = h1.shape[0]
    rows = nodes + 2 * REACH1
    n2 = nodes // 4
    edges = nodes * K
    shape = jax.ShapeDtypeStruct
    return pl.pallas_call(
        level1_kernel,
        out_shape=[
            shape((nodes, W), BF16),
            shape((n2 + 2 * REACH2, W), F32),
            shape((2 * REACH2, W), BF16),
            shape((2 * REACH2, W), BF16),
        ],
        in_specs=[pl.BlockSpec(memory_space=pltpu.SMEM)]
        + [vmem()] * 3
        + [anyspace()] * 3
        + [vmem()] * len(weights),
        out_specs=[vmem()] * 4,
        scratch_shapes=[
            pltpu.VMEM((rows, W), BF16),
            *gather_scratch(rows, nodes),
            pltpu.VMEM((UNROLL * C, W), BF16),
            *[pltpu.VMEM((W, W), BF16) for _ in range(5)],
            pltpu.SemaphoreType.DMA((UNROLL,)),
            pltpu.SemaphoreType.DMA((6,)),
        ],
        compiler_params=pltpu.CompilerParams(vmem_limit_bytes=VMEM_BYTES),
        cost_estimate=pl.CostEstimate(
            flops=4 * edges * W * W, bytes_accessed=rows * W * 4, transcendentals=edges * W
        ),
        name="level1",
    )(base, nbr_t, mask_t, owner2, h1, prev, nxt, *weights)


def level2_kernel(
    base_ref, nbr, mask, part, inner, outer, h2, near2, far2, u2, a2, b2, m2, v2, h2o, edge_in, edge_out,
    h2x, tab, dst, idx_vm, s0, s1, s2, s3, r0, r1, z, mc, mv, bh, fsem
):
    n2 = h2o.shape[0]
    rows = n2 + 2 * REACH2
    S = 2 * REACH2
    odd = is_odd(base_ref, n2)
    u = u2[...]
    for q in range(rows // S):
        piece = part[pl.ds(q * S, S), :]
        if q == 0:
            piece = piece + pick(odd, inner[...], outer[...])
        elif q == rows // S - 1:
            piece = piece + pick(odd, outer[...], inner[...])
        d = mm(piece.astype(BF16), u)
        for hf in range(2):
            at = q * S + hf * REACH2
            if at == 0:
                src = pick(odd, near2[...], far2[...])
            elif at == rows - REACH2:
                src = pick(odd, far2[...], near2[...])
            else:
                src = h2[pl.ds(at - REACH2, REACH2), :]
            dd = d[hf * REACH2 : (hf + 1) * REACH2]
            h2x[pl.ds(at, REACH2), :] = (src.astype(F32) + dd).astype(BF16)
    lane = lax.broadcasted_iota(jnp.int32, (K, L), 1)
    base = base_ref[0]
    for c in range(n2 // C):
        cols = slice(c * C, (c + 1) * C)
        row = nbr[:, cols] - (base - REACH2)
        idx_vm[c] = 2 * jnp.where(mask[:, cols] > 0, row, rows)
    mcv = centered(m2)
    mc[...] = mcv * (1.0 / 16.0)
    mv[...] = mm(mcv, v2[...]).astype(BF16)
    build_table(tab, h2x, half(a2), 0, rows)
    tab[pl.ds(2 * rows, 8), :] = jnp.full((8, L), DEAD, F32)
    bh[...] = half(b2)

    def receivers(pair):
        return mm(h2x[pl.ds(pl.multiple_of(pair * PAIR, PAIR) + REACH2, PAIR), :], bh[...])

    def post(step, at):
        node = pl.multiple_of(jnp.maximum(step, 0) * PAIR, PAIR)
        hrow = h2x[pl.ds(node + REACH2, PAIR), :].astype(F32)
        h2o[pl.ds(node, PAIR), :] = (hrow + mm(z[pl.ds(at * PAIR, PAIR), :], mv[...])).astype(BF16)

    edge_loop(
        n2 // C, idx_vm, (s0, s1, s2, s3), fsem, (r0, r1), tab, dst, mc, z, receivers, post, lambda p, at: None
    )
    low = h2o[pl.ds(0, REACH2), :]
    up = h2o[pl.ds(n2 - REACH2, REACH2), :]
    edge_in[...] = pick(odd, low, up).astype(BF16)
    edge_out[...] = pick(odd, up, low).astype(BF16)


def level2(base, nbr_t, mask_t, part, from_lo, from_hi, h2, lo2, hi2, weights):
    nodes = h2.shape[0]
    rows = nodes + 2 * REACH2
    args = (base, nbr_t, mask_t, part, from_lo, from_hi, h2, lo2, hi2, *weights)
    shape = jax.ShapeDtypeStruct
    return pl.pallas_call(
        level2_kernel,
        out_shape=[shape((nodes, W), BF16), shape((REACH2, W), BF16), shape((REACH2, W), BF16)],
        grid=(1,),
        in_specs=[pl.BlockSpec(memory_space=pltpu.SMEM)]
        + [vmem()] * 6
        + [pl.BlockSpec((REACH2, W), lambda t: (REACH1 // REACH2, 0))] * 2
        + [vmem()] * len(weights),
        out_specs=[vmem()] * 3,
        scratch_shapes=[
            pltpu.VMEM((rows, W), BF16),
            *gather_scratch(rows, nodes),
            *[pltpu.VMEM((W, W), BF16) for _ in range(3)],
            pltpu.SemaphoreType.DMA((UNROLL,)),
        ],
        compiler_params=pltpu.CompilerParams(vmem_limit_bytes=VMEM_BYTES),
        cost_estimate=pl.CostEstimate(
            flops=4 * nodes * K * W * W, bytes_accessed=rows * W * 4, transcendentals=nodes * K * W
        ),
        name="level2",
    )(*args)


DOWN = 2048
GROUP = 512


def down_kernel(base_ref, owner, h1a, h2o, near, far, a_down, b_down, m_down, o_ref, pd, bd, mdc):
    t = pl.program_id(0)
    n2 = h2o.shape[0]

    @pl.when(t == 0)
    def _():
        a = half(a_down)
        odd = is_odd(base_ref, n2)
        low = pick(odd, near[...], far[...]).astype(BF16)
        up = pick(odd, far[...], near[...]).astype(BF16)
        pd[pl.ds(0, REACH2), :] = mm(low, a).astype(BF16)
        for b in range(n2 // 256):
            pd[pl.ds(REACH2 + b * 256, 256), :] = mm(h2o[pl.ds(b * 256, 256), :], a).astype(BF16)
        pd[pl.ds(REACH2 + n2, REACH2), :] = mm(up, a).astype(BF16)
        bd[...] = half(b_down)
        mdc[...] = centered(m_down)

    win = GROUP // 4 + 2 * REACH2
    lane = lax.broadcasted_iota(jnp.int32, (L, L), 1).astype(F32)
    for g in range(DOWN // GROUP):
        start = t * (DOWN // 4) + g * (GROUP // 4)
        lowest = base_ref[0] + start - REACH2
        table = pd[pl.ds(pl.multiple_of(start, L), win), :]
        hot = []
        for j in range(GROUP // L):
            ow = owner[pl.ds(t * (DOWN // L) + g * (GROUP // L) + j, 1), :] - lowest
            col = jnp.transpose(jnp.broadcast_to(ow.astype(F32), (L, L)))
            hot.append(
                jnp.concatenate(
                    [jnp.where(col == lane + q * L, 1.0, 0.0).astype(BF16) for q in range(win // L)],
                    axis=1,
                )
            )
        hb = h1a[pl.ds(g * GROUP, GROUP), :]
        y = mm(jnp.concatenate(hot, axis=0), table) + mm(hb, bd[...])
        d = mm(act_of(y).astype(BF16), mdc[...])
        w = scale_of(d)
        ln = jnp.concatenate([d[:, :L] * w, d[:, L:] * w], axis=1)
        o_ref[pl.ds(g * GROUP, GROUP), :] = (hb.astype(F32) + ln).astype(BF16)


def down(base, owner2, h1a, h2o, lo, hi, a_down, b_down, m_down):
    nodes1 = h1a.shape[0]
    n2 = h2o.shape[0]

    def whole(shape):
        return pl.BlockSpec(shape, lambda t: (0, 0))

    block = pl.BlockSpec((DOWN, W), lambda t: (t, 0))
    return pl.pallas_call(
        down_kernel,
        grid=(nodes1 // DOWN,),
        out_shape=jax.ShapeDtypeStruct((nodes1, W), BF16),
        in_specs=[
            pl.BlockSpec(memory_space=pltpu.SMEM),
            whole(owner2.shape),
            block,
            whole((n2, W)),
            whole((REACH2, W)),
            whole((REACH2, W)),
            whole((W, W)),
            whole((W, W)),
            whole((W, W)),
        ],
        out_specs=block,
        scratch_shapes=[
            pltpu.VMEM((n2 + 2 * REACH2, W), BF16),
            pltpu.VMEM((W, W), BF16),
            pltpu.VMEM((W, W), BF16),
        ],
        compiler_params=pltpu.CompilerParams(vmem_limit_bytes=VMEM_BYTES),
        cost_estimate=pl.CostEstimate(
            flops=10 * nodes1 * W * W, bytes_accessed=nodes1 * W * 4, transcendentals=nodes1 * W
        ),
        name="down",
    )(base, owner2, h1a, h2o, lo, hi, a_down, b_down, m_down)


def swap(inner, outer, axis):
    count = lax.axis_size(axis)

    def both(first):
        pairs = [(i, i + 1) for i in range(first, count - 1, 2)]
        return pairs + [(j, i) for i, j in pairs]

    return lax.ppermute(inner, axis, both(0)), lax.ppermute(outer, axis, both(1))


def shards(
    h1,
    h2,
    nbr1,
    mask1,
    owner,
    nbr2,
    mask2,
    a1,
    b1,
    m1,
    u1,
    a_up,
    m_up,
    u2,
    a2,
    b2,
    m2,
    v2,
    a_down,
    b_down,
    m_down,
):
    nodes1 = h1.shape[0]
    nodes2 = h2.shape[0]
    device = lax.axis_index("grp") * lax.axis_size("sub") + lax.axis_index("sub")
    base = jnp.reshape(device * nodes2, (1,)).astype(jnp.int32)
    nbr1_t, mask1_t, nbr2_t, mask2_t = nbr1.T, mask1.T, nbr2.T, mask2.T
    owner2 = owner.reshape(nodes1 // L, L)
    up = jnp.concatenate([h1[nodes1 - REACH1 :], h2[nodes2 - REACH2 :]], axis=0)
    low = jnp.concatenate([h1[:REACH1], h2[:REACH2]], axis=0)
    odd = device % 2 == 1
    halo = swap(jnp.where(odd, low, up), jnp.where(odd, up, low), ("grp", "sub"))
    h1a, part, inner, outer = level1(
        base, nbr1_t, mask1_t, owner2, h1, *halo, (a1, b1, m1, u1, a_up, m_up)
    )
    inner, outer = swap(inner, outer, "sub")
    h2_out, edge_in, edge_out = level2(
        base, nbr2_t, mask2_t, part, inner, outer, h2, *halo, (u2, a2, b2, m2, v2)
    )
    edge_in, edge_out = swap(edge_in, edge_out, "sub")
    h1_out = down(base, owner2, h1a, h2_out, edge_in, edge_out, a_down, b_down, m_down)
    return (h1_out, h2_out)


def solution(mesh):
    split = P(("grp", "sub"), None)
    return jax.shard_map(
        shards,
        mesh=mesh,
        in_specs=(split, split, split, split, P(("grp", "sub")), split, split) + (P(),) * 14,
        out_specs=(split, split),
        check_vma=False,
    )
```
